128 devices in a mesh: tm: 16 (over z_hi, y, core), tensor: 8 (over x, z_lo).
Axes of the slice: x: 4, y: 4, z: 4 (z_hi: 2, z_lo: 2; z = z_hi * 2 + z_lo), core: 2. Of those that a mesh axis runs over, the one named last changes fastest.
Arguments:
- queries: bfloat16 [1024, 5120], P('tm', 'tensor'), may hold values from -150 to 150
- cached_keys: bfloat16 [65536, 5120], P('tm', 'tensor'), may hold values from -20 to 20
- cached_values: bfloat16 [65536, 5120], P('tm', 'tensor'), may hold values from -6 to 6
- out_weight: bfloat16 [5120, 5120], P('tensor'), may hold values from -0.078125 to 0.078125
Outputs:
- united: float32 [1024, 5120], P('tm', 'tensor')
The draws below stay inside these ranges and needn't reach their ends.
All inputs are finite; a program needn't handle non-finite values.
Results may differ from the reference program's by a relative error of at most 0.0044.
Values may be sent and summed in bfloat16 or wider, within the bound.
A program may use at most 128 MiB of HBM per device.

```python
import jax
import jax.numpy as jnp
from jax import lax

D = 5120
H = 40
HD = 128
QROWS = 1024
KV = 65536


def draw_queries(key, part):
    key = jax.random.fold_in(key, 1)
    pieces = jax.random.split(key, 1)
    drawn = 3.0 * jax.random.truncated_normal(pieces[0], -5.0, 5.0, (QROWS, H * HD), jnp.float32)
    return drawn.astype(jnp.bfloat16)


def draw_cached_keys(key, part):
    key = jax.random.fold_in(key, 2)
    pieces = jax.random.split(key, 1)
    drawn = jax.random.truncated_normal(pieces[0], -5.0, 5.0, (KV, H * HD), jnp.float32)
    return drawn.astype(jnp.bfloat16)


def steps_of(own_key, shape, cuts, low, high):
    loudness, own = 1.0, jax.random.fold_in(own_key, 6)
    for dim, blocks in cuts:
        steps = jnp.exp(jax.random.uniform(jax.random.fold_in(own, dim), (blocks,), jnp.float32, low / len(cuts), high / len(cuts)))
        loudness = loudness * jnp.repeat(steps, shape[dim] // blocks).reshape([-1 if axis == dim else 1 for axis in range(len(shape))])
    return loudness


def bell_draw(stream_key, shape, width, limit, shards=(), held_as=jnp.bfloat16):
    values = jax.random.normal(stream_key, shape, jnp.float32) * width
    if len(shards) > 0:
        values = steps_of(stream_key, shape, shards, -0.22, 0.18) * values
    return jnp.clip(values, min=-limit, max=limit).astype(held_as)


def setup_inputs(seed: int = 0) -> dict:
    key_of = jax.random.split(jax.random.key(seed), 5)
    return {
        "queries": draw_queries(jax.random.fold_in(key_of[4], 71), 0),
        "cached_keys": draw_cached_keys(jax.random.fold_in(key_of[4], 71), 0),
        "cached_values": bell_draw(key_of[2], (KV, H * HD), 1.0, 6.0, ((0, 16), (1, 8))),
        "out_weight": bell_draw(key_of[3], (H * HD, D), (H * HD) ** -0.5, 0.078125, ((0, 8),)),
    }


def reference(queries, cached_keys, cached_values, out_weight):
    scaling = 1.0 / (HD ** 0.5)
    query_heads = queries.reshape(QROWS, H, HD)
    key_heads = cached_keys.reshape(KV, H, HD)
    value_heads = cached_values.reshape(KV, H, HD)

    def one_head(head_index):
        query_head = lax.dynamic_index_in_dim(query_heads, head_index, 1, keepdims=False)
        key_head = lax.dynamic_index_in_dim(key_heads, head_index, 1, keepdims=False)
        value_head = lax.dynamic_index_in_dim(value_heads, head_index, 1, keepdims=False)
        scores = jnp.dot(query_head, key_head.T, preferred_element_type=jnp.float32) * scaling
        largest = jnp.max(scores, axis=1, keepdims=True)
        probs = jnp.exp(scores - largest)
        totals = jnp.sum(probs, axis=1, keepdims=True)
        summed = jnp.dot(probs, value_head.astype(jnp.float32), precision=lax.Precision.HIGHEST)
        return summed / totals

    per_head = lax.map(one_head, jnp.arange(H, dtype=jnp.int32))
    attended = jnp.transpose(per_head, (1, 0, 2)).reshape(QROWS, H * HD).astype(jnp.bfloat16)
    return jnp.dot(attended, out_weight, preferred_element_type=jnp.float32)
```

```python
import math

import jax
import jax.numpy as jnp
from jax import lax
from jax.experimental import pallas as pl
from jax.experimental.pallas import tpu as pltpu
from jax.sharding import PartitionSpec as P

HD = 128
LOG2E = 1.4426950408889634
MESH = pl.DeviceIdType.MESH
NT = (((1,), (1,)), ((), ()))
NN = (((1,), (0,)), ((), ()))
F32, BF = jnp.float32, jnp.bfloat16

ROWS = 512
KEYS = 256


def on_device(queries, cached_keys, cached_values, out_weight):
    n_tm, n_te = lax.axis_size("tm"), lax.axis_size("tensor")
    own = queries.shape[0]
    rows = own * n_tm
    kv = cached_keys.shape[0]
    width = cached_keys.shape[1]
    heads = width // HD
    model = out_weight.shape[1]
    feat = model // n_te
    tile = min(ROWS, rows)
    tiles = rows // tile
    per_tile = tile // own
    scale = LOG2E / math.sqrt(HD)
    groups = [(0, 1), (1, 2), (2, heads)]

    def kernel(q_hbm, k_hbm, v_hbm, w_hbm, out, qbuf, kbuf, vbuf, wbuf, sbuf, mbuf, osend, orecv,
               att, psend, precv, q_sem, k_sem, v_sem, w_sem, qs, qr, os, orr, ps, pr):
        tm, te = lax.axis_index("tm"), lax.axis_index("tensor")

        def hcol(h):
            return pl.ds(pl.multiple_of(h * HD, HD), HD)

        def block(i):
            return pl.ds(pl.multiple_of(i * own, own), own)

        def k_load(h):
            return pltpu.make_async_copy(k_hbm.at[:, hcol(h)], kbuf.at[h], k_sem.at[h])

        def v_load(h):
            return pltpu.make_async_copy(v_hbm.at[:, hcol(h)], vbuf.at[h, :, pl.ds(0, HD)], v_sem.at[h])

        q_load = pltpu.make_async_copy(q_hbm, qbuf.at[block(tm), :], q_sem)
        w_load = pltpu.make_async_copy(w_hbm, wbuf, w_sem)
        q_load.start()
        k_load(0).start()
        v_load(0).start()

        barrier = pltpu.get_barrier_semaphore()

        def greet_tm(d, _):
            pl.semaphore_signal(barrier, inc=1, device_id={"tm": lax.rem(tm + d, n_tm)}, device_id_type=MESH)
            return 0

        def greet_te(d, _):
            pl.semaphore_signal(barrier, inc=1, device_id={"tensor": lax.rem(te + d, n_te)}, device_id_type=MESH)
            return 0

        lax.fori_loop(1, n_tm, greet_tm, 0)
        lax.fori_loop(1, n_te, greet_te, 0)

        def ones(h):
            def fill(i, _):
                vbuf[h, pl.ds(pl.multiple_of(i * 256, 256), 256), HD:] = jnp.ones((256, HD), BF)
                return 0
            lax.fori_loop(0, kv // 256, fill, 0)

        ones(0)
        pl.semaphore_wait(barrier, n_tm - 1 + n_te - 1)

        def q_copy(g, d):
            lo, hi = groups[g]
            cols = pl.ds(lo * HD, (hi - lo) * HD)
            return pltpu.make_async_remote_copy(
                src_ref=q_hbm.at[:, cols], dst_ref=qbuf.at[block(tm), cols],
                send_sem=qs.at[g, d], recv_sem=qr.at[g, d],
                device_id={"tm": lax.rem(tm + d, n_tm)}, device_id_type=MESH)

        def q_arrival(g, d):
            lo, hi = groups[g]
            cols = pl.ds(lo * HD, (hi - lo) * HD)
            return pltpu.make_async_remote_copy(
                src_ref=q_hbm.at[:, cols], dst_ref=qbuf.at[block(lax.rem(tm + n_tm - d, n_tm)), cols],
                send_sem=qs.at[g, d], recv_sem=qr.at[g, d],
                device_id={"tm": lax.rem(tm + d, n_tm)}, device_id_type=MESH)

        for g in range(len(groups)):
            def send_q(d, _, g=g):
                q_copy(g, d).start()
                return 0
            lax.fori_loop(1, n_tm, send_q, 0)

        for h in range(1, heads):
            k_load(h).start()
            v_load(h).start()
        w_load.start()
        for h in range(1, heads):
            ones(h)
        q_load.wait()

        def need_queries(g):
            def wait_q(d, _):
                q_arrival(g, d).wait_recv()
                return 0
            lax.fori_loop(1, n_tm, wait_q, 0)

        def step(t, do_s, do_p):
            h, r = t // tiles, lax.rem(t, tiles)
            hn, rn = (t + 1) // tiles, lax.rem(t + 1, tiles)
            cur, nxt = lax.rem(t, 2), lax.rem(t + 1, 2)
            mx = acc = None
            if do_s:
                qn = qbuf[pl.ds(pl.multiple_of(rn * tile, tile), tile), hcol(hn)]
            if do_p:
                m = mbuf[cur][:, :1]
            for c in range(kv // KEYS):
                ck = slice(c * KEYS, (c + 1) * KEYS)
                if do_s:
                    x = lax.dot_general(qn, kbuf[hn, ck, :], NT, preferred_element_type=F32)
                    sbuf[nxt, :, ck] = x
                    y = x[:, :HD]
                    for i in range(1, KEYS // HD):
                        y = jnp.maximum(y, x[:, i * HD:(i + 1) * HD])
                    mx = y if mx is None else jnp.maximum(mx, y)
                if do_p:
                    p = jnp.exp2(sbuf[cur, :, ck] * scale - m).astype(BF)
                    d = lax.dot_general(p, vbuf[h, ck, :], NN, preferred_element_type=F32)
                    acc = d if acc is None else acc + d
            if do_p:
                total = acc[:, HD:]
                lse = mbuf[cur] + jnp.log(total) * LOG2E
                hi = lse.astype(BF).astype(F32)
                mid = (lse - hi).astype(BF).astype(F32)
                low = lse - hi - mid
                lane = lax.broadcasted_iota(jnp.int32, (tile, HD), 1)
                stats = jnp.where(lane == 0, hi, jnp.where(lane == 1, mid, jnp.where(lane == 2, low, 0.0)))
                trow = pl.ds(pl.multiple_of(r * tile, tile), tile)
                osend[h, trow, :HD] = (acc[:, :HD] / total).astype(BF)
                osend[h, trow, HD:] = stats.astype(BF)
            if do_s:
                mbuf[nxt] = jnp.broadcast_to(jnp.max(mx, axis=1, keepdims=True) * scale, (tile, HD))

        def o_copy(h, d):
            to = lax.rem(tm + d, n_tm)
            return pltpu.make_async_remote_copy(
                src_ref=osend.at[h, block(to), :], dst_ref=orecv.at[h, tm],
                send_sem=os.at[h, d], recv_sem=orr.at[h, d],
                device_id={"tm": to}, device_id_type=MESH)

        def o_arrival(h, d):
            return pltpu.make_async_remote_copy(
                src_ref=osend.at[h, block(tm), :], dst_ref=orecv.at[h, lax.rem(tm + n_tm - d, n_tm)],
                send_sem=os.at[h, d], recv_sem=orr.at[h, d],
                device_id={"tm": lax.rem(tm + d, n_tm)}, device_id_type=MESH)

        def send_tile(t):
            h, r = t // tiles, lax.rem(t, tiles)

            def one(j, _):
                to = r * per_tile + lax.rem(tm + 1 + j, per_tile)
                d = lax.rem(to - tm + n_tm, n_tm)

                @pl.when(to != tm)
                def _():
                    o_copy(h, d).start()
                return 0
            lax.fori_loop(0, per_tile, one, 0)

        def combine(h):
            def wait_o(d, _):
                o_arrival(h, d).wait_recv()
                return 0
            lax.fori_loop(1, n_tm, wait_o, 0)
            orecv[h, tm] = osend[h, block(tm), :]
            stats = orecv[h, :, :, HD:].reshape(rows, HD)
            lse = lax.dot_general(stats, jnp.ones((HD, HD), BF), NN, preferred_element_type=F32).reshape(n_tm, own, HD)
            w = jnp.exp2(lse - jnp.max(lse, axis=0, keepdims=True))
            num = jnp.sum(w * orecv[h, :, :, :HD].astype(F32), axis=0)
            att[:, hcol(h)] = (num / jnp.sum(w, axis=0)).astype(BF)

        last = heads * tiles - 1
        need_queries(0)
        k_load(0).wait()
        step(-1 + 0 * tm, True, False)

        def body(t, _):
            for g in range(1, len(groups)):
                @pl.when(t + 1 == groups[g][0] * tiles)
                def _():
                    need_queries(g)
            h, r = t // tiles, lax.rem(t, tiles)

            @pl.when(r == tiles - 1)
            def _():
                k_load(h + 1).wait()

            @pl.when(r == 0)
            def _():
                v_load(h).wait()

            step(t, True, True)
            send_tile(t)

            @pl.when(jnp.logical_and(h >= 1, r == tiles - 1))
            def _():
                combine(h - 1)
            return 0

        lax.fori_loop(0, last, body, 0)
        if tiles == 1:
            v_load(heads - 1).wait()
        step(last + 0 * tm, False, True)
        send_tile(last)
        w_load.wait()
        combine(heads - 2)
        combine(heads - 1)

        def fcol(i):
            return pl.ds(pl.multiple_of(i * feat, feat), feat)

        def p_copy(d):
            return pltpu.make_async_remote_copy(
                src_ref=psend.at[d], dst_ref=precv.at[d],
                send_sem=ps.at[d], recv_sem=pr.at[d],
                device_id={"tensor": lax.rem(te + d, n_te)}, device_id_type=MESH)

        def project(d, _):
            part = lax.dot_general(att[...], wbuf[:, fcol(lax.rem(te + d, n_te))], NN, preferred_element_type=F32)
            psend[d] = part.astype(BF)
            p_copy(d).start()
            return 0

        lax.fori_loop(1, n_te, project, 0)
        out[...] = lax.dot_general(att[...], wbuf[:, fcol(te)], NN, preferred_element_type=F32)

        def gather_p(d, _):
            p_copy(d).wait_recv()
            out[...] += precv[d].astype(F32)
            return 0

        lax.fori_loop(1, n_te, gather_p, 0)

        def sent_p(d, _):
            p_copy(d).wait_send()
            return 0

        lax.fori_loop(1, n_te, sent_p, 0)

        def sent_tm(d, _):
            for g in range(len(groups)):
                q_copy(g, d).wait_send()
            for h in range(heads):
                o_copy(h, d).wait_send()
            return 0

        lax.fori_loop(1, n_tm, sent_tm, 0)

    any_ = pl.BlockSpec(memory_space=pl.ANY)
    dma = pltpu.SemaphoreType.DMA
    return pl.pallas_call(
        kernel,
        out_shape=jax.ShapeDtypeStruct((own, feat), F32),
        in_specs=[any_] * 4,
        out_specs=pl.BlockSpec(memory_space=pltpu.VMEM),
        scratch_shapes=[
            pltpu.VMEM((rows, width), BF),
            pltpu.VMEM((heads, kv, HD), BF),
            pltpu.VMEM((heads, kv, 2 * HD), BF),
            pltpu.VMEM((width, model), BF),
            pltpu.VMEM((2, tile, kv), F32),
            pltpu.VMEM((2, tile, HD), F32),
            pltpu.VMEM((heads, rows, 2 * HD), BF),
            pltpu.VMEM((heads, n_tm, own, 2 * HD), BF),
            pltpu.VMEM((own, width), BF),
            pltpu.VMEM((n_te, own, feat), BF),
            pltpu.VMEM((n_te, own, feat), BF),
            dma, dma((heads,)), dma((heads,)), dma,
            dma((len(groups), n_tm)), dma((len(groups), n_tm)),
            dma((heads, n_tm)), dma((heads, n_tm)),
            dma((n_te,)), dma((n_te,)),
        ],
        compiler_params=pltpu.CompilerParams(
            collective_id=0, has_side_effects=True, vmem_limit_bytes=60 * 2**20),
        name="late_uniting_attention",
    )(queries, cached_keys, cached_values, out_weight)


def solution(mesh):
    placed = (P("tm", "tensor"), P("tm", "tensor"), P("tm", "tensor"), P("tensor", None))
    return jax.shard_map(
        on_device, mesh=mesh, in_specs=placed, out_specs=P("tm", "tensor"), check_vma=False
    )
```

```python
import math

import jax
import jax.numpy as jnp
from jax import lax
from jax.experimental import pallas as pl
from jax.experimental.pallas import tpu as pltpu
from jax.sharding import PartitionSpec as P

HD = 128
LOG2E = 1.4426950408889634
MESH = pl.DeviceIdType.MESH
NT = (((1,), (1,)), ((), ()))
NN = (((1,), (0,)), ((), ()))
F32, BF = jnp.float32, jnp.bfloat16

KEYS = 256
TILES = 2


def on_device(queries, cached_keys, cached_values, out_weight):
    n_tm, n_te = lax.axis_size("tm"), lax.axis_size("tensor")
    chips = n_tm // 2
    own = queries.shape[0]
    kv = cached_keys.shape[0]
    width = cached_keys.shape[1]
    heads = width // HD
    model = out_weight.shape[1]
    feat = model // n_te
    part = own // TILES
    half = part * chips
    tile = 2 * half
    steps = TILES * heads
    scale = LOG2E / math.sqrt(HD)
    groups = [(0, 0, 2), (0, 2, heads)] + [(r, 0, heads) for r in range(1, TILES)]

    def kernel(q_hbm, k_hbm, v_hbm, w_hbm, out, qbuf, kbuf, vbuf, wbuf, s_a, s_b, m_a, m_b, keep, give, taken,
               osend, orecv, att, psend, precv,
               q_sem, k_sem, v_sem, w_sem, qs, qr, fs, fr, gs, gr, os, orr, ps, pr):
        tm, te = lax.axis_index("tm"), lax.axis_index("tensor")
        core, chip = lax.rem(tm, 2), tm // 2
        sibling = tm + 1 - 2 * core

        def hcol(h):
            return pl.ds(pl.multiple_of(h * HD, HD), HD)

        def fcol(i):
            return pl.ds(pl.multiple_of(i * feat, feat), feat)

        def to_chip(d):
            return {"tm": 2 * lax.rem(chip + d, chips) + core}

        def to_group(d):
            return {"tensor": lax.rem(te + d, n_te)}

        def block(d):
            return pl.ds(pl.multiple_of(lax.rem(chip + chips - d, chips) * part, part), part)

        def each(lo, hi, f):
            def go(i, _):
                f(i)
                return 0
            lax.fori_loop(lo, hi, go, 0)

        def k_load(h):
            return pltpu.make_async_copy(k_hbm.at[:, hcol(h)], kbuf.at[h], k_sem.at[h])

        def v_load(h):
            return pltpu.make_async_copy(v_hbm.at[:, hcol(h)], vbuf.at[h, :, pl.ds(0, HD)], v_sem.at[h])

        def q_load(r):
            return pltpu.make_async_copy(q_hbm.at[pl.ds(r * part, part), :], qbuf.at[r, block(0), :], q_sem.at[r])

        w_load = pltpu.make_async_copy(w_hbm, wbuf, w_sem)
        for r in range(TILES):
            q_load(r).start()
        for h in range(heads):
            k_load(h).start()
            v_load(h).start()
        w_load.start()

        barrier = pltpu.get_barrier_semaphore()
        pl.semaphore_signal(barrier, inc=1, device_id={"tm": sibling}, device_id_type=MESH)
        each(1, chips, lambda d: pl.semaphore_signal(barrier, inc=1, device_id=to_chip(d), device_id_type=MESH))
        each(1, n_te, lambda d: pl.semaphore_signal(barrier, inc=1, device_id=to_group(d), device_id_type=MESH))

        def fill(i):
            for h in range(heads):
                vbuf[h, pl.ds(pl.multiple_of(i * 256, 256), 256), HD:] = jnp.ones((256, HD), BF)

        each(0, kv // 256, fill)
        for r in range(TILES):
            q_load(r).wait()
        pl.semaphore_wait(barrier, 1 + chips - 1 + n_te - 1)

        def q_copy(g, d, at):
            r, lo, hi = groups[g]
            cols = pl.ds(lo * HD, (hi - lo) * HD)
            return pltpu.make_async_remote_copy(
                src_ref=q_hbm.at[pl.ds(r * part, part), cols], dst_ref=qbuf.at[r, block(at), cols],
                send_sem=qs.at[g, d], recv_sem=qr.at[g, d], device_id=to_chip(d), device_id_type=MESH)

        def q_pass(g):
            r, lo, hi = groups[g]
            cols = pl.ds(lo * HD, (hi - lo) * HD)
            return pltpu.make_async_remote_copy(
                src_ref=qbuf.at[r, pl.ds(0, half), cols], dst_ref=qbuf.at[r, pl.ds(half, half), cols],
                send_sem=fs.at[g], recv_sem=fr.at[g], device_id={"tm": sibling}, device_id_type=MESH)

        def q_send(g):
            each(1, chips, lambda d: q_copy(g, d, 0).start())

        def q_relay(g):
            each(1, chips, lambda d: q_copy(g, d, d).wait_recv())
            q_pass(g).start()

        def step(t, cur, nxt, mcur, mnxt):
            h = lax.rem(t, heads)
            hn, rn = lax.rem(t + 1, heads), (t + 1) // heads
            mx = acc = None
            if nxt is not None:
                qn = qbuf[rn, :, hcol(hn)]
            if cur is not None:
                m = mcur[:, :1]
            for c in range(kv // KEYS):
                ck = slice(c * KEYS, (c + 1) * KEYS)
                if nxt is not None:
                    x = lax.dot_general(qn, kbuf[hn, ck, :], NT, preferred_element_type=F32)
                    nxt[:, ck] = x
                    y = x[:, :HD]
                    for i in range(1, KEYS // HD):
                        y = jnp.maximum(y, x[:, i * HD:(i + 1) * HD])
                    mx = y if mx is None else jnp.maximum(mx, y)
                if cur is not None:
                    p = jnp.exp2(cur[:, ck] * scale - m).astype(BF)
                    d = lax.dot_general(p, vbuf[h, ck, :], NN, preferred_element_type=F32)
                    acc = d if acc is None else acc + d
            if cur is not None:
                total = acc[:, HD:]
                lse = mcur[...] + jnp.log(total) * LOG2E
                mean = acc[:, :HD] / total
                keep[t, :, :HD] = mean[:half]
                keep[t, :, HD:] = lse[:half]
                give[t, :, :HD] = mean[half:]
                give[t, :, HD:] = lse[half:]
                to_sibling(t).start()
            if nxt is not None:
                mnxt[...] = jnp.broadcast_to(jnp.max(mx, axis=1, keepdims=True) * scale, (tile, HD))

        def to_sibling(t):
            return pltpu.make_async_remote_copy(
                src_ref=give.at[t], dst_ref=taken.at[t], send_sem=gs.at[t], recv_sem=gr.at[t],
                device_id={"tm": sibling}, device_id_type=MESH)

        def o_copy(t, d, at):
            return pltpu.make_async_remote_copy(
                src_ref=osend.at[t, lax.rem(chip + d, chips)], dst_ref=orecv.at[t, lax.rem(chip + chips - at, chips)],
                send_sem=os.at[t, d], recv_sem=orr.at[t, d], device_id=to_chip(d), device_id_type=MESH)

        def merge(t):
            to_sibling(t).wait_recv()
            la, lb = keep[t, :, HD:], taken[t, :, HD:]
            top = jnp.maximum(la, lb)
            wa, wb = jnp.exp2(la - top), jnp.exp2(lb - top)
            total = wa + wb
            mean = (wa * keep[t, :, :HD] + wb * taken[t, :, :HD]) / total
            lse = top + jnp.log(total) * LOG2E
            hi = lse.astype(BF).astype(F32)
            mid = (lse - hi).astype(BF).astype(F32)
            low = lse - hi - mid
            lane = lax.broadcasted_iota(jnp.int32, (half, HD), 1)
            stats = jnp.where(lane == 0, hi, jnp.where(lane == 1, mid, jnp.where(lane == 2, low, 0.0)))
            osend[t, :, :, :HD] = mean.astype(BF).reshape(chips, part, HD)
            osend[t, :, :, HD:] = stats.astype(BF).reshape(chips, part, HD)
            each(1, chips, lambda d: o_copy(t, d, 0).start())
            orecv[t, chip] = osend[t, chip]

        def combine(t):
            each(1, chips, lambda d: o_copy(t, d, d).wait_recv())
            stats = orecv[t, :, :, HD:].reshape(half, HD)
            lse = lax.dot_general(stats, jnp.ones((HD, HD), BF), NN, preferred_element_type=F32)
            lse = lse.reshape(chips, part, HD)
            w = jnp.exp2(lse - jnp.max(lse, axis=0, keepdims=True))
            num = jnp.sum(w * orecv[t, :, :, :HD].astype(F32), axis=0)
            att[t // heads, :, hcol(lax.rem(t, heads))] = (num / jnp.sum(w, axis=0)).astype(BF)

        def p_copy(r, d):
            return pltpu.make_async_remote_copy(
                src_ref=psend.at[r, d], dst_ref=precv.at[r, d], send_sem=ps.at[r, d], recv_sem=pr.at[r, d],
                device_id=to_group(d), device_id_type=MESH)

        def project(r):
            def share(d):
                product = lax.dot_general(
                    att[r], wbuf[:, fcol(lax.rem(te + d, n_te))], NN, preferred_element_type=F32)
                psend[r, d] = product.astype(BF)
                p_copy(r, d).start()
            each(1, n_te, share)
            out[r * part:(r + 1) * part, :] = lax.dot_general(
                att[r], wbuf[:, fcol(te)], NN, preferred_element_type=F32)

        def unite(r):
            def add(d):
                p_copy(r, d).wait_recv()
                out[r * part:(r + 1) * part, :] += precv[r, d].astype(F32)
            each(1, n_te, add)

        def before(t):
            h, hn = lax.rem(t, heads), lax.rem(t + 1, heads)
            for g in range(1, len(groups)):
                r, lo, _ = groups[g]

                @pl.when(t + 1 == r * heads + lo)
                def _(g=g):
                    q_pass(g).wait_recv()

            @pl.when(t + 1 < heads)
            def _():
                k_load(hn).wait()

            @pl.when(t < heads)
            def _():
                v_load(h).wait()

        def after(t):
            for g in range(1, len(groups)):
                @pl.when(t == g - 1)
                def _(g=g):
                    q_relay(g)

            @pl.when(t >= 1)
            def _():
                merge(t - 1)

            @pl.when(t >= 2)
            def _():
                combine(t - 2)

            for r in range(TILES - 1):
                @pl.when(t == (r + 1) * heads + 1)
                def _(r=r):
                    if r == 0:
                        w_load.wait()
                    project(r)

        q_send(0)
        q_relay(0)
        for g in range(1, len(groups)):
            q_send(g)
        k_load(0).wait()
        q_pass(0).wait_recv()
        step(0 * tm - 1, None, s_a, None, m_a)

        def pair(u, _):
            before(2 * u)
            step(2 * u, s_a, s_b, m_a, m_b)
            after(2 * u)
            before(2 * u + 1)
            step(2 * u + 1, s_b, s_a, m_b, m_a)
            after(2 * u + 1)
            return 0

        last = 0 * tm + steps - 1
        lax.fori_loop(0, (steps - 1) // 2, pair, 0)
        if steps % 2 == 0:
            before(last - 1)
            step(last - 1, s_a, s_b, m_a, m_b)
            after(last - 1)
        end = (s_b, m_b) if steps % 2 == 0 else (s_a, m_a)
        before(last)
        step(last, end[0], None, end[1], None)
        after(last)
        merge(last)
        combine(last - 1)
        combine(last)
        if TILES == 1:
            w_load.wait()
        project(TILES - 1)
        for r in range(TILES):
            unite(r)

        def sent(d):
            for g in range(len(groups)):
                q_copy(g, d, 0).wait_send()
            each(0, steps, lambda t: o_copy(t, d, 0).wait_send())

        each(1, chips, sent)
        for g in range(len(groups)):
            q_pass(g).wait_send()
        each(0, steps, lambda t: to_sibling(t).wait_send())
        for r in range(TILES):
            each(1, n_te, lambda d: p_copy(r, d).wait_send())

    any_ = pl.BlockSpec(memory_space=pl.ANY)
    dma = pltpu.SemaphoreType.DMA
    n_g = len(groups)
    return pl.pallas_call(
        kernel,
        out_shape=jax.ShapeDtypeStruct((own, feat), F32),
        in_specs=[any_] * 4,
        out_specs=pl.BlockSpec(memory_space=pltpu.VMEM),
        scratch_shapes=[
            pltpu.VMEM((TILES, tile, width), BF),
            pltpu.VMEM((heads, kv, HD), BF),
            pltpu.VMEM((heads, kv, 2 * HD), BF),
            pltpu.VMEM((width, model), BF),
            pltpu.VMEM((tile, kv), F32),
            pltpu.VMEM((tile, kv), F32),
            pltpu.VMEM((tile, HD), F32),
            pltpu.VMEM((tile, HD), F32),
            pltpu.VMEM((steps, half, 2 * HD), F32),
            pltpu.VMEM((steps, half, 2 * HD), F32),
            pltpu.VMEM((steps, half, 2 * HD), F32),
            pltpu.VMEM((steps, chips, part, 2 * HD), BF),
            pltpu.VMEM((steps, chips, part, 2 * HD), BF),
            pltpu.VMEM((TILES, part, width), BF),
            pltpu.VMEM((TILES, n_te, part, feat), BF),
            pltpu.VMEM((TILES, n_te, part, feat), BF),
            dma((TILES,)), dma((heads,)), dma((heads,)), dma,
            dma((n_g, chips)), dma((n_g, chips)), dma((n_g,)), dma((n_g,)),
            dma((steps,)), dma((steps,)),
            dma((steps, chips)), dma((steps, chips)),
            dma((TILES, n_te)), dma((TILES, n_te)),
        ],
        compiler_params=pltpu.CompilerParams(
            collective_id=0, has_side_effects=True, vmem_limit_bytes=60 * 2**20),
        name="late_uniting_attention",
    )(queries, cached_keys, cached_values, out_weight)


def solution(mesh):
    placed = (P("tm", "tensor"), P("tm", "tensor"), P("tm", "tensor"), P("tensor", None))
    return jax.shard_map(
        on_device, mesh=mesh, in_specs=placed, out_specs=P("tm", "tensor"), check_vma=False
    )
```

```python
import math

import jax
import jax.numpy as jnp
from jax import lax
from jax.experimental import pallas as pl
from jax.experimental.pallas import tpu as pltpu
from jax.sharding import PartitionSpec as P

HD = 128
LOG2E = 1.4426950408889634
MESH = pl.DeviceIdType.MESH
NT = (((1,), (1,)), ((), ()))
NN = (((1,), (0,)), ((), ()))
F32, BF = jnp.float32, jnp.bfloat16

KEYS = 256
TILES = 2
LAG = 3


def on_device(queries, cached_keys, cached_values, out_weight):
    n_tm, n_te = lax.axis_size("tm"), lax.axis_size("tensor")
    chips = n_tm // 2
    own = queries.shape[0]
    kv = cached_keys.shape[0]
    width = cached_keys.shape[1]
    heads = width // HD
    model = out_weight.shape[1]
    feat = model // n_te
    part = own // TILES
    half = part * chips
    tile = 2 * half
    steps = TILES * heads
    scale = LOG2E / math.sqrt(HD)
    groups = [(0, 0, 1), (0, 1, 2), (0, 2, heads)] + [(r, 0, heads) for r in range(1, TILES)]
    direct = 3

    def kernel(q_hbm, k_hbm, v_hbm, w_hbm, out, qbuf, kbuf, vbuf, wbuf, s_a, s_b, m_a, m_b, keep, give, taken,
               osend, orecv, att, shares, psend, precv,
               q_sem, k_sem, v_sem, w_sem, qs, qr, xs, xr, fs, fr, gs, gr, os, orr, ps, pr):
        tm, te = lax.axis_index("tm"), lax.axis_index("tensor")
        core, chip = lax.rem(tm, 2), tm // 2
        sibling = tm + 1 - 2 * core

        def hcol(h):
            return pl.ds(pl.multiple_of(h * HD, HD), HD)

        def fcol(i):
            return pl.ds(pl.multiple_of(i * feat, feat), feat)

        def to_chip(d):
            return {"tm": 2 * lax.rem(chip + d, chips) + core}

        def to_group(d):
            return {"tensor": lax.rem(te + d, n_te)}

        def block(d):
            return pl.ds(pl.multiple_of(lax.rem(chip + chips - d, chips) * part, part), part)

        def each(lo, hi, f):
            def go(i, _):
                f(i)
                return 0
            lax.fori_loop(lo, hi, go, 0)

        def k_load(h):
            return pltpu.make_async_copy(k_hbm.at[:, hcol(h)], kbuf.at[h], k_sem.at[h])

        def v_load(h):
            return pltpu.make_async_copy(v_hbm.at[:, hcol(h)], vbuf.at[h, :, pl.ds(0, HD)], v_sem.at[h])

        def q_load(r):
            return pltpu.make_async_copy(q_hbm.at[pl.ds(r * part, part), :], qbuf.at[r, block(0), :], q_sem.at[r])

        w_load = pltpu.make_async_copy(w_hbm, wbuf, w_sem)
        for r in range(TILES):
            q_load(r).start()
        for h in range(heads):
            k_load(h).start()
            v_load(h).start()
        w_load.start()

        barrier = pltpu.get_barrier_semaphore()
        pl.semaphore_signal(barrier, inc=1, device_id={"tm": sibling}, device_id_type=MESH)
        each(1, chips, lambda d: pl.semaphore_signal(barrier, inc=1, device_id=to_chip(d), device_id_type=MESH))
        each(1, chips, lambda d: pl.semaphore_signal(
            barrier, inc=1, device_id={"tm": 2 * lax.rem(chip + d, chips) + 1 - core}, device_id_type=MESH))
        each(1, n_te, lambda d: pl.semaphore_signal(barrier, inc=1, device_id=to_group(d), device_id_type=MESH))

        def fill(i):
            for h in range(heads):
                vbuf[h, pl.ds(pl.multiple_of(i * 256, 256), 256), HD:] = jnp.ones((256, HD), BF)

        each(0, kv // 256, fill)
        for r in range(TILES):
            q_load(r).wait()
        pl.semaphore_wait(barrier, n_tm - 1 + n_te - 1)

        def q_copy(g, d, at):
            r, lo, hi = groups[g]
            cols = pl.ds(lo * HD, (hi - lo) * HD)
            return pltpu.make_async_remote_copy(
                src_ref=q_hbm.at[pl.ds(r * part, part), cols], dst_ref=qbuf.at[r, block(at), cols],
                send_sem=qs.at[g, d], recv_sem=qr.at[g, d], device_id=to_chip(d), device_id_type=MESH)

        def q_cross(g, d, at):
            r, lo, hi = groups[g]
            cols = pl.ds(lo * HD, (hi - lo) * HD)
            place = pl.ds(pl.multiple_of(half + lax.rem(chip + chips - at, chips) * part, part), part)
            return pltpu.make_async_remote_copy(
                src_ref=q_hbm.at[pl.ds(r * part, part), cols], dst_ref=qbuf.at[r, place, cols],
                send_sem=xs.at[g, d], recv_sem=xr.at[g, d],
                device_id={"tm": 2 * lax.rem(chip + d, chips) + 1 - core}, device_id_type=MESH)

        def q_pass(g):
            r, lo, hi = groups[g]
            cols = pl.ds(lo * HD, (hi - lo) * HD)
            return pltpu.make_async_remote_copy(
                src_ref=qbuf.at[r, pl.ds(0, half), cols], dst_ref=qbuf.at[r, pl.ds(half, half), cols],
                send_sem=fs.at[g], recv_sem=fr.at[g], device_id={"tm": sibling}, device_id_type=MESH)

        def q_send(g):
            if g < direct:
                q_cross(g, 0, 0).start()

            def one(d):
                q_copy(g, d, 0).start()
                if g < direct:
                    q_cross(g, d, 0).start()
            each(1, chips, one)

        def q_need(g):
            if g < direct:
                each(1, chips, lambda d: q_copy(g, d, d).wait_recv())
                each(0, chips, lambda d: q_cross(g, d, d).wait_recv())
            else:
                q_pass(g).wait_recv()

        def q_relay(g):
            each(1, chips, lambda d: q_copy(g, d, d).wait_recv())
            q_pass(g).start()

        def step(t, cur, nxt, mcur, mnxt):
            h = lax.rem(t, heads)
            hn, rn = lax.rem(t + 1, heads), (t + 1) // heads
            mx = acc = None
            if nxt is not None:
                qn = qbuf[rn, :, hcol(hn)]
            if cur is not None:
                m = mcur[:, :1]
            for c in range(kv // KEYS):
                ck = slice(c * KEYS, (c + 1) * KEYS)
                if nxt is not None:
                    x = lax.dot_general(qn, kbuf[hn, ck, :], NT, preferred_element_type=F32)
                    nxt[:, ck] = x
                    y = x[:, :HD]
                    for i in range(1, KEYS // HD):
                        y = jnp.maximum(y, x[:, i * HD:(i + 1) * HD])
                    mx = y if mx is None else jnp.maximum(mx, y)
                if cur is not None:
                    p = jnp.exp2(cur[:, ck] * scale - m).astype(BF)
                    d = lax.dot_general(p, vbuf[h, ck, :], NN, preferred_element_type=F32)
                    acc = d if acc is None else acc + d
            if cur is not None:
                total = acc[:, HD:]
                lse = mcur[...] + jnp.log(total) * LOG2E
                mean = acc[:, :HD] / total
                keep[t, :, :HD] = mean[:half]
                keep[t, :, HD:] = lse[:half]
                give[t, :, :HD] = mean[half:]
                give[t, :, HD:] = lse[half:]
                to_sibling(t).start()
            if nxt is not None:
                mnxt[...] = jnp.broadcast_to(jnp.max(mx, axis=1, keepdims=True) * scale, (tile, HD))

        def to_sibling(t):
            return pltpu.make_async_remote_copy(
                src_ref=give.at[t], dst_ref=taken.at[t], send_sem=gs.at[t], recv_sem=gr.at[t],
                device_id={"tm": sibling}, device_id_type=MESH)

        def o_copy(t, d, at):
            return pltpu.make_async_remote_copy(
                src_ref=osend.at[t, lax.rem(chip + d, chips)], dst_ref=orecv.at[t, lax.rem(chip + chips - at, chips)],
                send_sem=os.at[t, d], recv_sem=orr.at[t, d], device_id=to_chip(d), device_id_type=MESH)

        def merge(t):
            to_sibling(t).wait_recv()
            la, lb = keep[t, :, HD:], taken[t, :, HD:]
            top = jnp.maximum(la, lb)
            wa, wb = jnp.exp2(la - top), jnp.exp2(lb - top)
            total = wa + wb
            mean = (wa * keep[t, :, :HD] + wb * taken[t, :, :HD]) / total
            lse = top + jnp.log(total) * LOG2E
            hi = lse.astype(BF).astype(F32)
            mid = (lse - hi).astype(BF).astype(F32)
            low = lse - hi - mid
            lane = lax.broadcasted_iota(jnp.int32, (half, HD), 1)
            stats = jnp.where(lane == 0, hi, jnp.where(lane == 1, mid, jnp.where(lane == 2, low, 0.0)))
            osend[t, :, :, :HD] = mean.astype(BF).reshape(chips, part, HD)
            osend[t, :, :, HD:] = stats.astype(BF).reshape(chips, part, HD)
            each(1, chips, lambda d: o_copy(t, d, 0).start())
            orecv[t, chip] = osend[t, chip]

        def combine(t):
            each(1, chips, lambda d: o_copy(t, d, d).wait_recv())
            stats = orecv[t, :, :, HD:].reshape(half, HD)
            lse = lax.dot_general(stats, jnp.ones((HD, HD), BF), NN, preferred_element_type=F32)
            lse = lse.reshape(chips, part, HD)
            w = jnp.exp2(lse - jnp.max(lse, axis=0, keepdims=True))
            num = jnp.sum(w * orecv[t, :, :, :HD].astype(F32), axis=0)
            att[t // heads, :, hcol(lax.rem(t, heads))] = (num / jnp.sum(w, axis=0)).astype(BF)

        def p_copy(r, d):
            return pltpu.make_async_remote_copy(
                src_ref=psend.at[r, d], dst_ref=precv.at[r, d], send_sem=ps.at[r, d], recv_sem=pr.at[r, d],
                device_id=to_group(d), device_id_type=MESH)

        most = width - HD

        def prepare(r):
            def share(d):
                shares[d] = lax.dot_general(
                    att[r, :, :most], wbuf[:most, fcol(lax.rem(te + d, n_te))], NN, preferred_element_type=F32)
            each(0, n_te, share)

        def project(r):
            def product(d):
                return shares[d] + lax.dot_general(
                    att[r, :, most:], wbuf[most:, fcol(lax.rem(te + d, n_te))], NN, preferred_element_type=F32)

            def share(d):
                psend[r, d] = product(d).astype(BF)
                p_copy(r, d).start()
            each(1, n_te, share)
            out[r * part:(r + 1) * part, :] = product(0)

        def unite(r):
            def add(d):
                p_copy(r, d).wait_recv()
                out[r * part:(r + 1) * part, :] += precv[r, d].astype(F32)
            each(1, n_te, add)

        def before(t):
            h, hn = lax.rem(t, heads), lax.rem(t + 1, heads)
            for g in range(1, len(groups)):
                r, lo, _ = groups[g]

                @pl.when(t + 1 == r * heads + lo)
                def _(g=g):
                    q_need(g)

            @pl.when(t + 1 < heads)
            def _():
                k_load(hn).wait()

            @pl.when(t < heads)
            def _():
                v_load(h).wait()

        def after(t):
            for g in range(direct, len(groups)):
                @pl.when(t == (groups[g][0] - 1) * heads + 1)
                def _(g=g):
                    q_relay(g)

            @pl.when(t >= 1)
            def _():
                merge(t - 1)

            @pl.when(t >= LAG)
            def _():
                combine(t - LAG)

            for r in range(TILES - 1):
                @pl.when(t == (r + 1) * heads - 1 + LAG)
                def _(r=r):
                    if r == 0:
                        w_load.wait()
                    prepare(r)
                    project(r)

        q_send(0)
        q_send(1)
        k_load(0).wait()
        q_need(0)
        for g in range(2, len(groups)):
            q_send(g)
        step(0 * tm - 1, None, s_a, None, m_a)

        def pair(u, _):
            before(2 * u)
            step(2 * u, s_a, s_b, m_a, m_b)
            after(2 * u)
            before(2 * u + 1)
            step(2 * u + 1, s_b, s_a, m_b, m_a)
            after(2 * u + 1)
            return 0

        last = 0 * tm + steps - 1
        lax.fori_loop(0, (steps - 1) // 2, pair, 0)
        if steps % 2 == 0:
            before(last - 1)
            step(last - 1, s_a, s_b, m_a, m_b)
            after(last - 1)
        end = (s_b, m_b) if steps % 2 == 0 else (s_a, m_a)
        before(last)
        step(last, end[0], None, end[1], None)
        after(last)
        merge(last)
        for i in range(LAG - 1, 0, -1):
            combine(last - i)
        prepare(TILES - 1)
        combine(last)
        project(TILES - 1)
        for r in range(TILES):
            unite(r)

        def sent(d):
            for g in range(len(groups)):
                q_copy(g, d, 0).wait_send()
                if g < direct:
                    q_cross(g, d, 0).wait_send()
            each(0, steps, lambda t: o_copy(t, d, 0).wait_send())

        each(1, chips, sent)
        for g in range(len(groups)):
            if g < direct:
                q_cross(g, 0, 0).wait_send()
            else:
                q_pass(g).wait_send()
        each(0, steps, lambda t: to_sibling(t).wait_send())
        for r in range(TILES):
            each(1, n_te, lambda d: p_copy(r, d).wait_send())

    any_ = pl.BlockSpec(memory_space=pl.ANY)
    dma = pltpu.SemaphoreType.DMA
    n_g = len(groups)
    return pl.pallas_call(
        kernel,
        out_shape=jax.ShapeDtypeStruct((own, feat), F32),
        in_specs=[any_] * 4,
        out_specs=pl.BlockSpec(memory_space=pltpu.VMEM),
        scratch_shapes=[
            pltpu.VMEM((TILES, tile, width), BF),
            pltpu.VMEM((heads, kv, HD), BF),
            pltpu.VMEM((heads, kv, 2 * HD), BF),
            pltpu.VMEM((width, model), BF),
            pltpu.VMEM((tile, kv), F32),
            pltpu.VMEM((tile, kv), F32),
            pltpu.VMEM((tile, HD), F32),
            pltpu.VMEM((tile, HD), F32),
            pltpu.VMEM((steps, half, 2 * HD), F32),
            pltpu.VMEM((steps, half, 2 * HD), F32),
            pltpu.VMEM((steps, half, 2 * HD), F32),
            pltpu.VMEM((steps, chips, part, 2 * HD), BF),
            pltpu.VMEM((steps, chips, part, 2 * HD), BF),
            pltpu.VMEM((TILES, part, width), BF),
            pltpu.VMEM((n_te, part, feat), F32),
            pltpu.VMEM((TILES, n_te, part, feat), BF),
            pltpu.VMEM((TILES, n_te, part, feat), BF),
            dma((TILES,)), dma((heads,)), dma((heads,)), dma,
            dma((n_g, chips)), dma((n_g, chips)), dma((n_g, chips)), dma((n_g, chips)), dma((n_g,)), dma((n_g,)),
            dma((steps,)), dma((steps,)),
            dma((steps, chips)), dma((steps, chips)),
            dma((TILES, n_te)), dma((TILES, n_te)),
        ],
        compiler_params=pltpu.CompilerParams(
            collective_id=0, has_side_effects=True, vmem_limit_bytes=60 * 2**20),
        name="late_uniting_attention",
    )(queries, cached_keys, cached_values, out_weight)


def solution(mesh):
    placed = (P("tm", "tensor"), P("tm", "tensor"), P("tm", "tensor"), P("tensor", None))
    return jax.shard_map(
        on_device, mesh=mesh, in_specs=placed, out_specs=P("tm", "tensor"), check_vma=False
    )
```

```python
import math

import jax
import jax.numpy as jnp
from jax import lax
from jax.experimental import pallas as pl
from jax.experimental.pallas import tpu as pltpu
from jax.sharding import PartitionSpec as P

HD = 128
LOG2E = 1.4426950408889634
MESH = pl.DeviceIdType.MESH
NT = (((1,), (1,)), ((), ()))
NN = (((1,), (0,)), ((), ()))
F32, BF = jnp.float32, jnp.bfloat16

KEYS = 256
TILES = 2
LAG = 3


def on_device(queries, cached_keys, cached_values, out_weight):
    n_tm, n_te = lax.axis_size("tm"), lax.axis_size("tensor")
    chips = n_tm // 2
    own = queries.shape[0]
    kv = cached_keys.shape[0]
    width = cached_keys.shape[1]
    heads = width // HD
    model = out_weight.shape[1]
    feat = model // n_te
    part = own // TILES
    half = part * chips
    tile = 2 * half
    steps = TILES * heads
    scale = LOG2E / math.sqrt(HD)
    groups = [(0, h, h + 1) for h in range(heads)] + [(r, 0, heads) for r in range(1, TILES)]
    direct = heads

    def kernel(q_hbm, k_hbm, v_hbm, w_hbm, out, qbuf, kbuf, vbuf, wbuf, s_a, s_b, m_a, m_b, keep, give, taken,
               osend, orecv, att, shares, psend, precv,
               q_sem, k_sem, v_sem, w_sem, qs, qr, xs, xr, fs, fr, gs, gr, os, orr, ps, pr):
        tm, te = lax.axis_index("tm"), lax.axis_index("tensor")
        core, chip = lax.rem(tm, 2), tm // 2
        sibling = tm + 1 - 2 * core

        def hcol(h):
            return pl.ds(pl.multiple_of(h * HD, HD), HD)

        def fcol(i):
            return pl.ds(pl.multiple_of(i * feat, feat), feat)

        def to_chip(d):
            return {"tm": 2 * lax.rem(chip + d, chips) + core}

        def to_group(d):
            return {"tensor": lax.rem(te + d, n_te)}

        def block(d):
            return pl.ds(pl.multiple_of(lax.rem(chip + chips - d, chips) * part, part), part)

        def each(lo, hi, f):
            def go(i, _):
                f(i)
                return 0
            lax.fori_loop(lo, hi, go, 0)

        def k_load(h):
            return pltpu.make_async_copy(k_hbm.at[:, hcol(h)], kbuf.at[h], k_sem.at[h])

        def v_load(h):
            return pltpu.make_async_copy(v_hbm.at[:, hcol(h)], vbuf.at[h, :, pl.ds(0, HD)], v_sem.at[h])

        def q_load(r):
            return pltpu.make_async_copy(q_hbm.at[pl.ds(r * part, part), :], qbuf.at[r, block(0), :], q_sem.at[r])

        w_load = pltpu.make_async_copy(w_hbm, wbuf, w_sem)
        for r in range(TILES):
            q_load(r).start()
        for h in range(heads):
            k_load(h).start()
            v_load(h).start()
        w_load.start()

        barrier = pltpu.get_barrier_semaphore()
        pl.semaphore_signal(barrier, inc=1, device_id={"tm": sibling}, device_id_type=MESH)
        each(1, chips, lambda d: pl.semaphore_signal(barrier, inc=1, device_id=to_chip(d), device_id_type=MESH))
        each(1, chips, lambda d: pl.semaphore_signal(
            barrier, inc=1, device_id={"tm": 2 * lax.rem(chip + d, chips) + 1 - core}, device_id_type=MESH))
        each(1, n_te, lambda d: pl.semaphore_signal(barrier, inc=1, device_id=to_group(d), device_id_type=MESH))

        def fill(i):
            for h in range(heads):
                vbuf[h, pl.ds(pl.multiple_of(i * 256, 256), 256), HD:] = jnp.ones((256, HD), BF)

        each(0, kv // 256, fill)
        for r in range(TILES):
            q_load(r).wait()
        pl.semaphore_wait(barrier, n_tm - 1 + n_te - 1)

        def q_copy(g, d, at):
            r, lo, hi = groups[g]
            cols = pl.ds(lo * HD, (hi - lo) * HD)
            return pltpu.make_async_remote_copy(
                src_ref=q_hbm.at[pl.ds(r * part, part), cols], dst_ref=qbuf.at[r, block(at), cols],
                send_sem=qs.at[g, d], recv_sem=qr.at[g, d], device_id=to_chip(d), device_id_type=MESH)

        def q_cross(g, d, at):
            r, lo, hi = groups[g]
            cols = pl.ds(lo * HD, (hi - lo) * HD)
            place = pl.ds(pl.multiple_of(half + lax.rem(chip + chips - at, chips) * part, part), part)
            return pltpu.make_async_remote_copy(
                src_ref=q_hbm.at[pl.ds(r * part, part), cols], dst_ref=qbuf.at[r, place, cols],
                send_sem=xs.at[g, d], recv_sem=xr.at[g, d],
                device_id={"tm": 2 * lax.rem(chip + d, chips) + 1 - core}, device_id_type=MESH)

        def q_pass(g):
            r, lo, hi = groups[g]
            cols = pl.ds(lo * HD, (hi - lo) * HD)
            return pltpu.make_async_remote_copy(
                src_ref=qbuf.at[r, pl.ds(0, half), cols], dst_ref=qbuf.at[r, pl.ds(half, half), cols],
                send_sem=fs.at[g], recv_sem=fr.at[g], device_id={"tm": sibling}, device_id_type=MESH)

        def q_send(g):
            if g < direct:
                q_cross(g, 0, 0).start()

            def one(d):
                q_copy(g, d, 0).start()
                if g < direct:
                    q_cross(g, d, 0).start()
            each(1, chips, one)

        def q_need(g):
            if g < direct:
                each(1, chips, lambda d: q_copy(g, d, d).wait_recv())
                each(0, chips, lambda d: q_cross(g, d, d).wait_recv())
            else:
                q_pass(g).wait_recv()

        def q_relay(g):
            each(1, chips, lambda d: q_copy(g, d, d).wait_recv())
            q_pass(g).start()

        def step(t, cur, nxt, mcur, mnxt):
            h = lax.rem(t, heads)
            hn, rn = lax.rem(t + 1, heads), (t + 1) // heads
            mx, acc = [None, None], [None, None]
            parts = [slice(0, half), slice(half, tile)]
            for c in range(kv // KEYS):
                ck = slice(c * KEYS, (c + 1) * KEYS)
                for i, rs in enumerate(parts):
                    if nxt is not None:
                        qn = qbuf[rn, rs, hcol(hn)]
                        x = lax.dot_general(qn, kbuf[hn, ck, :], NT, preferred_element_type=F32)
                        nxt[rs, ck] = x
                        y = x[:, :HD]
                        for n in range(1, KEYS // HD):
                            y = jnp.maximum(y, x[:, n * HD:(n + 1) * HD])
                        mx[i] = y if c == 0 else jnp.maximum(mx[i], y)
                    if cur is not None:
                        p = jnp.exp2(cur[rs, ck] * scale - mcur[rs, :1]).astype(BF)
                        d = lax.dot_general(p, vbuf[h, ck, :], NN, preferred_element_type=F32)
                        acc[i] = d if c == 0 else acc[i] + d
            if cur is not None:
                for i, put in ((1, give), (0, keep)):
                    total = acc[i][:, HD:]
                    put[t, :, :HD] = acc[i][:, :HD] / total
                    put[t, :, HD:] = mcur[parts[i], :] + jnp.log(total) * LOG2E
                to_sibling(t).start()
            if nxt is not None:
                for i, rs in enumerate(parts):
                    mnxt[rs, :] = jnp.broadcast_to(jnp.max(mx[i], axis=1, keepdims=True) * scale, (half, HD))

        def to_sibling(t):
            return pltpu.make_async_remote_copy(
                src_ref=give.at[t], dst_ref=taken.at[t], send_sem=gs.at[t], recv_sem=gr.at[t],
                device_id={"tm": sibling}, device_id_type=MESH)

        def o_copy(t, d, at):
            return pltpu.make_async_remote_copy(
                src_ref=osend.at[t, lax.rem(chip + d, chips)], dst_ref=orecv.at[t, lax.rem(chip + chips - at, chips)],
                send_sem=os.at[t, d], recv_sem=orr.at[t, d], device_id=to_chip(d), device_id_type=MESH)

        def merge(t):
            to_sibling(t).wait_recv()
            la, lb = keep[t, :, HD:], taken[t, :, HD:]
            top = jnp.maximum(la, lb)
            wa, wb = jnp.exp2(la - top), jnp.exp2(lb - top)
            total = wa + wb
            mean = (wa * keep[t, :, :HD] + wb * taken[t, :, :HD]) / total
            lse = top + jnp.log(total) * LOG2E
            hi = lse.astype(BF).astype(F32)
            mid = (lse - hi).astype(BF).astype(F32)
            low = lse - hi - mid
            lane = lax.broadcasted_iota(jnp.int32, (half, HD), 1)
            stats = jnp.where(lane == 0, hi, jnp.where(lane == 1, mid, jnp.where(lane == 2, low, 0.0)))
            osend[t, :, :, :HD] = mean.astype(BF).reshape(chips, part, HD)
            osend[t, :, :, HD:] = stats.astype(BF).reshape(chips, part, HD)
            each(1, chips, lambda d: o_copy(t, d, 0).start())
            orecv[t, chip] = osend[t, chip]

        def combine(t):
            each(1, chips, lambda d: o_copy(t, d, d).wait_recv())
            stats = orecv[t, :, :, HD:].reshape(half, HD)
            lse = lax.dot_general(stats, jnp.ones((HD, HD), BF), NN, preferred_element_type=F32)
            lse = lse.reshape(chips, part, HD)
            w = jnp.exp2(lse - jnp.max(lse, axis=0, keepdims=True))
            num = jnp.sum(w * orecv[t, :, :, :HD].astype(F32), axis=0)
            att[t // heads, :, hcol(lax.rem(t, heads))] = (num / jnp.sum(w, axis=0)).astype(BF)

        def p_copy(r, d):
            return pltpu.make_async_remote_copy(
                src_ref=psend.at[r, d], dst_ref=precv.at[r, d], send_sem=ps.at[r, d], recv_sem=pr.at[r, d],
                device_id=to_group(d), device_id_type=MESH)

        most = width - HD

        def prepare(r):
            def share(d):
                shares[d] = lax.dot_general(
                    att[r, :, :most], wbuf[:most, fcol(lax.rem(te + d, n_te))], NN, preferred_element_type=F32)
            each(0, n_te, share)

        def project(r):
            def product(d):
                return shares[d] + lax.dot_general(
                    att[r, :, most:], wbuf[most:, fcol(lax.rem(te + d, n_te))], NN, preferred_element_type=F32)

            def share(d):
                psend[r, d] = product(d).astype(BF)
                p_copy(r, d).start()
            each(1, n_te, share)
            out[r * part:(r + 1) * part, :] = product(0)

        def unite(r):
            def add(d):
                p_copy(r, d).wait_recv()
                out[r * part:(r + 1) * part, :] += precv[r, d].astype(F32)
            each(1, n_te, add)

        def before(t):
            h, hn = lax.rem(t, heads), lax.rem(t + 1, heads)
            for g in range(1, len(groups)):
                r, lo, _ = groups[g]

                @pl.when(t + 1 == r * heads + lo)
                def _(g=g):
                    q_need(g)

            @pl.when(t + 1 < heads)
            def _():
                k_load(hn).wait()

            @pl.when(t < heads)
            def _():
                v_load(h).wait()

        def after(t):
            for g in range(direct, len(groups)):
                @pl.when(t == (groups[g][0] - 1) * heads + 1)
                def _(g=g):
                    q_relay(g)

            @pl.when(t >= 1)
            def _():
                merge(t - 1)

            @pl.when(t >= LAG)
            def _():
                combine(t - LAG)

            for r in range(TILES - 1):
                @pl.when(t == (r + 1) * heads - 1 + LAG)
                def _(r=r):
                    if r == 0:
                        w_load.wait()
                    prepare(r)
                    project(r)

        for g in range(len(groups)):
            q_send(g)
        k_load(0).wait()
        q_need(0)
        step(0 * tm - 1, None, s_a, None, m_a)

        def pair(u, _):
            before(2 * u)
            step(2 * u, s_a, s_b, m_a, m_b)
            after(2 * u)
            before(2 * u + 1)
            step(2 * u + 1, s_b, s_a, m_b, m_a)
            after(2 * u + 1)
            return 0

        last = 0 * tm + steps - 1
        lax.fori_loop(0, (steps - 1) // 2, pair, 0)
        if steps % 2 == 0:
            before(last - 1)
            step(last - 1, s_a, s_b, m_a, m_b)
            after(last - 1)
        end = (s_b, m_b) if steps % 2 == 0 else (s_a, m_a)
        before(last)
        step(last, end[0], None, end[1], None)
        after(last)
        merge(last)
        for i in range(LAG - 1, 0, -1):
            combine(last - i)
        prepare(TILES - 1)
        for r in range(TILES - 1):
            unite(r)
        combine(last)
        project(TILES - 1)

        def sent(d):
            for g in range(len(groups)):
                q_copy(g, d, 0).wait_send()
                if g < direct:
                    q_cross(g, d, 0).wait_send()
            each(0, steps, lambda t: o_copy(t, d, 0).wait_send())

        each(1, chips, sent)
        for g in range(len(groups)):
            if g < direct:
                q_cross(g, 0, 0).wait_send()
            else:
                q_pass(g).wait_send()
        each(0, steps, lambda t: to_sibling(t).wait_send())
        unite(TILES - 1)
        for r in range(TILES):
            each(1, n_te, lambda d: p_copy(r, d).wait_send())

    any_ = pl.BlockSpec(memory_space=pl.ANY)
    dma = pltpu.SemaphoreType.DMA
    n_g = len(groups)
    return pl.pallas_call(
        kernel,
        out_shape=jax.ShapeDtypeStruct((own, feat), F32),
        in_specs=[any_] * 4,
        out_specs=pl.BlockSpec(memory_space=pltpu.VMEM),
        scratch_shapes=[
            pltpu.VMEM((TILES, tile, width), BF),
            pltpu.VMEM((heads, kv, HD), BF),
            pltpu.VMEM((heads, kv, 2 * HD), BF),
            pltpu.VMEM((width, model), BF),
            pltpu.VMEM((tile, kv), F32),
            pltpu.VMEM((tile, kv), F32),
            pltpu.VMEM((tile, HD), F32),
            pltpu.VMEM((tile, HD), F32),
            pltpu.VMEM((steps, half, 2 * HD), F32),
            pltpu.VMEM((steps, half, 2 * HD), F32),
            pltpu.VMEM((steps, half, 2 * HD), F32),
            pltpu.VMEM((steps, chips, part, 2 * HD), BF),
            pltpu.VMEM((steps, chips, part, 2 * HD), BF),
            pltpu.VMEM((TILES, part, width), BF),
            pltpu.VMEM((n_te, part, feat), F32),
            pltpu.VMEM((TILES, n_te, part, feat), BF),
            pltpu.VMEM((TILES, n_te, part, feat), BF),
            dma((TILES,)), dma((heads,)), dma((heads,)), dma,
            dma((n_g, chips)), dma((n_g, chips)), dma((n_g, chips)), dma((n_g, chips)), dma((n_g,)), dma((n_g,)),
            dma((steps,)), dma((steps,)),
            dma((steps, chips)), dma((steps, chips)),
            dma((TILES, n_te)), dma((TILES, n_te)),
        ],
        compiler_params=pltpu.CompilerParams(
            collective_id=0, has_side_effects=True, vmem_limit_bytes=60 * 2**20),
        name="late_uniting_attention",
    )(queries, cached_keys, cached_values, out_weight)


def solution(mesh):
    placed = (P("tm", "tensor"), P("tm", "tensor"), P("tm", "tensor"), P("tensor", None))
    return jax.shard_map(
        on_device, mesh=mesh, in_specs=placed, out_specs=P("tm", "tensor"), check_vma=False
    )
```

```python
import math

import jax
import jax.numpy as jnp
from jax import lax
from jax.experimental import pallas as pl
from jax.experimental.pallas import tpu as pltpu
from jax.sharding import PartitionSpec as P

HD = 128
LOG2E = 1.4426950408889634
MESH = pl.DeviceIdType.MESH
NT = (((1,), (1,)), ((), ()))
NN = (((1,), (0,)), ((), ()))
F32, BF = jnp.float32, jnp.bfloat16

KEYS = 256
TILES = 2
LAG = 3


def on_device(queries, cached_keys, cached_values, out_weight):
    n_tm, n_te = lax.axis_size("tm"), lax.axis_size("tensor")
    chips = n_tm // 2
    own = queries.shape[0]
    kv = cached_keys.shape[0]
    width = cached_keys.shape[1]
    heads = width // HD
    model = out_weight.shape[1]
    feat = model // n_te
    part = own // TILES
    half = part * chips
    tile = 2 * half
    steps = TILES * heads
    scale = LOG2E / math.sqrt(HD)
    groups = [(0, h, h + 1) for h in range(heads)] + [(r, 0, heads) for r in range(1, TILES)]
    direct = heads

    def kernel(q_hbm, k_hbm, v_hbm, w_hbm, out, qbuf, kbuf, vbuf, wbuf, s_a, s_b, m_a, m_b, keep, give, taken,
               osend, orecv, att, shares, psend, precv,
               q_sem, k_sem, v_sem, w_sem, qs, qr, xs, xr, fs, fr, gs, gr, os, orr, ps, pr):
        tm, te = lax.axis_index("tm"), lax.axis_index("tensor")
        core, chip = lax.rem(tm, 2), tm // 2
        sibling = tm + 1 - 2 * core

        def hcol(h):
            return pl.ds(pl.multiple_of(h * HD, HD), HD)

        def fcol(i):
            return pl.ds(pl.multiple_of(i * feat, feat), feat)

        def to_chip(d):
            return {"tm": 2 * lax.rem(chip + d, chips) + core}

        def to_group(d):
            return {"tensor": lax.rem(te + d, n_te)}

        def block(d):
            return pl.ds(pl.multiple_of(lax.rem(chip + chips - d, chips) * part, part), part)

        def each(lo, hi, f):
            def go(i, _):
                f(i)
                return 0
            lax.fori_loop(lo, hi, go, 0)

        def k_load(h):
            return pltpu.make_async_copy(k_hbm.at[:, hcol(h)], kbuf.at[h], k_sem.at[h])

        def v_load(h):
            return pltpu.make_async_copy(v_hbm.at[:, hcol(h)], vbuf.at[h, :, pl.ds(0, HD)], v_sem.at[h])

        def q_load(r):
            return pltpu.make_async_copy(q_hbm.at[pl.ds(r * part, part), :], qbuf.at[r, block(0), :], q_sem.at[r])

        w_load = pltpu.make_async_copy(w_hbm, wbuf, w_sem)
        for r in range(TILES):
            q_load(r).start()
        for h in range(heads):
            k_load(h).start()
            v_load(h).start()
        w_load.start()

        barrier = pltpu.get_barrier_semaphore()
        pl.semaphore_signal(barrier, inc=1, device_id={"tm": sibling}, device_id_type=MESH)
        each(1, chips, lambda d: pl.semaphore_signal(barrier, inc=1, device_id=to_chip(d), device_id_type=MESH))
        each(1, chips, lambda d: pl.semaphore_signal(
            barrier, inc=1, device_id={"tm": 2 * lax.rem(chip + d, chips) + 1 - core}, device_id_type=MESH))
        each(1, n_te, lambda d: pl.semaphore_signal(barrier, inc=1, device_id=to_group(d), device_id_type=MESH))

        def fill(i):
            for h in range(heads):
                vbuf[h, pl.ds(pl.multiple_of(i * 256, 256), 256), HD:] = jnp.ones((256, HD), BF)

        each(0, kv // 256, fill)
        for r in range(TILES):
            q_load(r).wait()
        pl.semaphore_wait(barrier, n_tm - 1 + n_te - 1)

        def q_copy(g, d, at):
            r, lo, hi = groups[g]
            cols = pl.ds(lo * HD, (hi - lo) * HD)
            return pltpu.make_async_remote_copy(
                src_ref=q_hbm.at[pl.ds(r * part, part), cols], dst_ref=qbuf.at[r, block(at), cols],
                send_sem=qs.at[g, d], recv_sem=qr.at[g, d], device_id=to_chip(d), device_id_type=MESH)

        def q_cross(g, d, at):
            r, lo, hi = groups[g]
            cols = pl.ds(lo * HD, (hi - lo) * HD)
            place = pl.ds(pl.multiple_of(half + lax.rem(chip + chips - at, chips) * part, part), part)
            return pltpu.make_async_remote_copy(
                src_ref=q_hbm.at[pl.ds(r * part, part), cols], dst_ref=qbuf.at[r, place, cols],
                send_sem=xs.at[g, d], recv_sem=xr.at[g, d],
                device_id={"tm": 2 * lax.rem(chip + d, chips) + 1 - core}, device_id_type=MESH)

        def q_pass(g):
            r, lo, hi = groups[g]
            cols = pl.ds(lo * HD, (hi - lo) * HD)
            return pltpu.make_async_remote_copy(
                src_ref=qbuf.at[r, pl.ds(0, half), cols], dst_ref=qbuf.at[r, pl.ds(half, half), cols],
                send_sem=fs.at[g], recv_sem=fr.at[g], device_id={"tm": sibling}, device_id_type=MESH)

        def q_send(g):
            if g < direct:
                q_cross(g, 0, 0).start()

            def one(d):
                q_copy(g, d, 0).start()
                if g < direct:
                    q_cross(g, d, 0).start()
            each(1, chips, one)

        def q_need(g):
            if g < direct:
                each(1, chips, lambda d: q_copy(g, d, d).wait_recv())
                each(0, chips, lambda d: q_cross(g, d, d).wait_recv())
            else:
                q_pass(g).wait_recv()

        def q_relay(g):
            each(1, chips, lambda d: q_copy(g, d, d).wait_recv())
            q_pass(g).start()

        def step(t, cur, nxt, mcur, mnxt):
            h = lax.rem(t, heads)
            hn, rn = lax.rem(t + 1, heads), (t + 1) // heads
            mx, acc = [None, None], [None, None]
            parts = [slice(0, half), slice(half, tile)]
            for c in range(kv // KEYS):
                ck = slice(c * KEYS, (c + 1) * KEYS)
                for i, rs in enumerate(parts):
                    if nxt is not None:
                        qn = qbuf[rn, rs, hcol(hn)]
                        x = lax.dot_general(qn, kbuf[hn, ck, :], NT, preferred_element_type=F32)
                        nxt[rs, ck] = x
                        y = x[:, :HD]
                        for n in range(1, KEYS // HD):
                            y = jnp.maximum(y, x[:, n * HD:(n + 1) * HD])
                        mx[i] = y if c == 0 else jnp.maximum(mx[i], y)
                    if cur is not None:
                        p = jnp.exp2(cur[rs, ck] * scale - mcur[rs, :1]).astype(BF)
                        d = lax.dot_general(p, vbuf[h, ck, :], NN, preferred_element_type=F32)
                        acc[i] = d if c == 0 else acc[i] + d
            if cur is not None:
                for i, put in ((1, give), (0, keep)):
                    total = acc[i][:, HD:]
                    put[t, :, :HD] = acc[i][:, :HD] / total
                    put[t, :, HD:] = mcur[parts[i], :] + jnp.log(total) * LOG2E
                to_sibling(t).start()
            if nxt is not None:
                for i, rs in enumerate(parts):
                    mnxt[rs, :] = jnp.broadcast_to(jnp.max(mx[i], axis=1, keepdims=True) * scale, (half, HD))

        def to_sibling(t):
            return pltpu.make_async_remote_copy(
                src_ref=give.at[t], dst_ref=taken.at[t], send_sem=gs.at[t], recv_sem=gr.at[t],
                device_id={"tm": sibling}, device_id_type=MESH)

        def o_copy(t, d, at):
            return pltpu.make_async_remote_copy(
                src_ref=osend.at[t, lax.rem(chip + d, chips)], dst_ref=orecv.at[t, lax.rem(chip + chips - at, chips)],
                send_sem=os.at[t, d], recv_sem=orr.at[t, d], device_id=to_chip(d), device_id_type=MESH)

        def merge(t):
            to_sibling(t).wait_recv()
            la, lb = keep[t, :, HD:], taken[t, :, HD:]
            top = jnp.maximum(la, lb)
            wa, wb = jnp.exp2(la - top), jnp.exp2(lb - top)
            total = wa + wb
            mean = (wa * keep[t, :, :HD] + wb * taken[t, :, :HD]) / total
            lse = top + jnp.log(total) * LOG2E
            hi = lse.astype(BF).astype(F32)
            mid = (lse - hi).astype(BF).astype(F32)
            low = lse - hi - mid
            lane = lax.broadcasted_iota(jnp.int32, (half, HD), 1)
            stats = jnp.where(lane == 0, hi, jnp.where(lane == 1, mid, jnp.where(lane == 2, low, 0.0)))
            osend[t, :, :, :HD] = mean.astype(BF).reshape(chips, part, HD)
            osend[t, :, :, HD:] = stats.astype(BF).reshape(chips, part, HD)
            each(1, chips, lambda d: o_copy(t, d, 0).start())
            orecv[t, chip] = osend[t, chip]

        def combine(t):
            each(1, chips, lambda d: o_copy(t, d, d).wait_recv())
            stats = orecv[t, :, :, HD:].reshape(half, HD)
            lse = lax.dot_general(stats, jnp.ones((HD, HD), BF), NN, preferred_element_type=F32)
            lse = lse.reshape(chips, part, HD)
            w = jnp.exp2(lse - jnp.max(lse, axis=0, keepdims=True))
            num = jnp.sum(w * orecv[t, :, :, :HD].astype(F32), axis=0)
            att[t // heads, :, hcol(lax.rem(t, heads))] = (num / jnp.sum(w, axis=0)).astype(BF)

        def p_copy(r, d):
            return pltpu.make_async_remote_copy(
                src_ref=psend.at[r, d], dst_ref=precv.at[r, d], send_sem=ps.at[r, d], recv_sem=pr.at[r, d],
                device_id=to_group(d), device_id_type=MESH)

        most = width - HD

        def prepare(r):
            def share(d):
                shares[d] = lax.dot_general(
                    att[r, :, :most], wbuf[:most, fcol(lax.rem(te + d, n_te))], NN, preferred_element_type=F32)
            each(0, n_te, share)

        def project(r):
            def product(d):
                return shares[d] + lax.dot_general(
                    att[r, :, most:], wbuf[most:, fcol(lax.rem(te + d, n_te))], NN, preferred_element_type=F32)

            def share(d):
                psend[r, d] = product(d).astype(BF)
                p_copy(r, d).start()
            each(1, n_te, share)
            out[r * part:(r + 1) * part, :] = product(0)

        def unite(r):
            def add(d):
                p_copy(r, d).wait_recv()
                out[r * part:(r + 1) * part, :] += precv[r, d].astype(F32)
            each(1, n_te, add)

        def before(t):
            h, hn = lax.rem(t, heads), lax.rem(t + 1, heads)
            for g in range(1, len(groups)):
                r, lo, _ = groups[g]

                @pl.when(t + 1 == r * heads + lo)
                def _(g=g):
                    q_need(g)

            @pl.when(t + 1 < heads)
            def _():
                k_load(hn).wait()

            @pl.when(t < heads)
            def _():
                v_load(h).wait()

        def after(t):
            for g in range(direct, len(groups)):
                @pl.when(t == (groups[g][0] - 1) * heads + 1)
                def _(g=g):
                    q_relay(g)

            @pl.when(t >= 1)
            def _():
                merge(t - 1)

            @pl.when(t >= LAG)
            def _():
                combine(t - LAG)

        for g in range(len(groups)):
            q_send(g)
        k_load(0).wait()
        q_need(0)
        step(0 * tm - 1, None, s_a, None, m_a)

        def pair(u, _):
            before(2 * u)
            step(2 * u, s_a, s_b, m_a, m_b)
            after(2 * u)
            before(2 * u + 1)
            step(2 * u + 1, s_b, s_a, m_b, m_a)
            after(2 * u + 1)
            return 0

        last = 0 * tm + steps - 1
        lax.fori_loop(0, (steps - 1) // 2, pair, 0)
        if steps % 2 == 0:
            before(last - 1)
            step(last - 1, s_a, s_b, m_a, m_b)
            after(last - 1)
        end = (s_b, m_b) if steps % 2 == 0 else (s_a, m_a)
        before(last)
        step(last, end[0], None, end[1], None)
        after(last)
        merge(last)
        w_load.wait()
        for r in range(TILES - 1):
            prepare(r)
            project(r)
        for i in range(LAG - 1, 0, -1):
            combine(last - i)
        prepare(TILES - 1)
        combine(last)
        project(TILES - 1)

        def sent(d):
            for g in range(len(groups)):
                q_copy(g, d, 0).wait_send()
                if g < direct:
                    q_cross(g, d, 0).wait_send()
            each(0, steps, lambda t: o_copy(t, d, 0).wait_send())

        each(1, chips, sent)
        for g in range(len(groups)):
            if g < direct:
                q_cross(g, 0, 0).wait_send()
            else:
                q_pass(g).wait_send()
        each(0, steps, lambda t: to_sibling(t).wait_send())
        for r in range(TILES):
            unite(r)
        for r in range(TILES):
            each(1, n_te, lambda d: p_copy(r, d).wait_send())

    any_ = pl.BlockSpec(memory_space=pl.ANY)
    dma = pltpu.SemaphoreType.DMA
    n_g = len(groups)
    return pl.pallas_call(
        kernel,
        out_shape=jax.ShapeDtypeStruct((own, feat), F32),
        in_specs=[any_] * 4,
        out_specs=pl.BlockSpec(memory_space=pltpu.VMEM),
        scratch_shapes=[
            pltpu.VMEM((TILES, tile, width), BF),
            pltpu.VMEM((heads, kv, HD), BF),
            pltpu.VMEM((heads, kv, 2 * HD), BF),
            pltpu.VMEM((width, model), BF),
            pltpu.VMEM((tile, kv), F32),
            pltpu.VMEM((tile, kv), F32),
            pltpu.VMEM((tile, HD), F32),
            pltpu.VMEM((tile, HD), F32),
            pltpu.VMEM((steps, half, 2 * HD), F32),
            pltpu.VMEM((steps, half, 2 * HD), F32),
            pltpu.VMEM((steps, half, 2 * HD), F32),
            pltpu.VMEM((steps, chips, part, 2 * HD), BF),
            pltpu.VMEM((steps, chips, part, 2 * HD), BF),
            pltpu.VMEM((TILES, part, width), BF),
            pltpu.VMEM((n_te, part, feat), F32),
            pltpu.VMEM((TILES, n_te, part, feat), BF),
            pltpu.VMEM((TILES, n_te, part, feat), BF),
            dma((TILES,)), dma((heads,)), dma((heads,)), dma,
            dma((n_g, chips)), dma((n_g, chips)), dma((n_g, chips)), dma((n_g, chips)), dma((n_g,)), dma((n_g,)),
            dma((steps,)), dma((steps,)),
            dma((steps, chips)), dma((steps, chips)),
            dma((TILES, n_te)), dma((TILES, n_te)),
        ],
        compiler_params=pltpu.CompilerParams(
            collective_id=0, has_side_effects=True, vmem_limit_bytes=60 * 2**20),
        name="late_uniting_attention",
    )(queries, cached_keys, cached_values, out_weight)


def solution(mesh):
    placed = (P("tm", "tensor"), P("tm", "tensor"), P("tm", "tensor"), P("tensor", None))
    return jax.shard_map(
        on_device, mesh=mesh, in_specs=placed, out_specs=P("tm", "tensor"), check_vma=False
    )
```

```python
import math

import jax
import jax.numpy as jnp
from jax import lax
from jax.experimental import pallas as pl
from jax.experimental.pallas import tpu as pltpu
from jax.sharding import PartitionSpec as P

HD = 128
LOG2E = 1.4426950408889634
MESH = pl.DeviceIdType.MESH
NT = (((1,), (1,)), ((), ()))
NN = (((1,), (0,)), ((), ()))
F32, BF = jnp.float32, jnp.bfloat16

KEYS = 256
TILES = 2
LAG = 3


def on_device(queries, cached_keys, cached_values, out_weight):
    n_tm, n_te = lax.axis_size("tm"), lax.axis_size("tensor")
    chips = n_tm // 2
    own = queries.shape[0]
    kv = cached_keys.shape[0]
    width = cached_keys.shape[1]
    heads = width // HD
    model = out_weight.shape[1]
    feat = model // n_te
    part = own // TILES
    half = part * chips
    tile = 2 * half
    steps = TILES * heads
    scale = LOG2E / math.sqrt(HD)
    groups = [(0, h, h + 1) for h in range(3)] + [(0, 3, heads)] + [(r, 0, heads) for r in range(1, TILES)]
    relay_at = {g: max(0, r * heads + lo - 3) for g, (r, lo, _) in enumerate(groups)}
    direct = 3

    def kernel(q_hbm, k_hbm, v_hbm, w_hbm, out, qbuf, kbuf, vbuf, wbuf, s_a, s_b, m_a, m_b, keep, give, taken,
               osend, orecv, att, shares, psend, precv,
               q_sem, k_sem, v_sem, w_sem, qs, qr, xs, xr, fs, fr, gs, gr, os, orr, ps, pr):
        tm, te = lax.axis_index("tm"), lax.axis_index("tensor")
        core, chip = lax.rem(tm, 2), tm // 2
        sibling = tm + 1 - 2 * core

        def hcol(h):
            return pl.ds(pl.multiple_of(h * HD, HD), HD)

        def fcol(i):
            return pl.ds(pl.multiple_of(i * feat, feat), feat)

        def to_chip(d):
            return {"tm": 2 * lax.rem(chip + d, chips) + core}

        def to_group(d):
            return {"tensor": lax.rem(te + d, n_te)}

        def block(d):
            return pl.ds(pl.multiple_of(lax.rem(chip + chips - d, chips) * part, part), part)

        def each(lo, hi, f):
            def go(i, _):
                f(i)
                return 0
            lax.fori_loop(lo, hi, go, 0)

        def k_load(h):
            return pltpu.make_async_copy(k_hbm.at[:, hcol(h)], kbuf.at[h], k_sem.at[h])

        def v_load(h):
            return pltpu.make_async_copy(v_hbm.at[:, hcol(h)], vbuf.at[h, :, pl.ds(0, HD)], v_sem.at[h])

        def q_load(r):
            return pltpu.make_async_copy(q_hbm.at[pl.ds(r * part, part), :], qbuf.at[r, block(0), :], q_sem.at[r])

        w_load = pltpu.make_async_copy(w_hbm, wbuf, w_sem)
        for r in range(TILES):
            q_load(r).start()
        for h in range(heads):
            k_load(h).start()
            v_load(h).start()
        w_load.start()

        barrier = pltpu.get_barrier_semaphore()
        pl.semaphore_signal(barrier, inc=1, device_id={"tm": sibling}, device_id_type=MESH)
        each(1, chips, lambda d: pl.semaphore_signal(barrier, inc=1, device_id=to_chip(d), device_id_type=MESH))
        each(1, chips, lambda d: pl.semaphore_signal(
            barrier, inc=1, device_id={"tm": 2 * lax.rem(chip + d, chips) + 1 - core}, device_id_type=MESH))
        each(1, n_te, lambda d: pl.semaphore_signal(barrier, inc=1, device_id=to_group(d), device_id_type=MESH))

        def fill(i):
            for h in range(heads):
                vbuf[h, pl.ds(pl.multiple_of(i * 256, 256), 256), HD:] = jnp.ones((256, HD), BF)

        each(0, kv // 256, fill)
        for r in range(TILES):
            q_load(r).wait()
        pl.semaphore_wait(barrier, n_tm - 1 + n_te - 1)

        def q_copy(g, d, at):
            r, lo, hi = groups[g]
            cols = pl.ds(lo * HD, (hi - lo) * HD)
            return pltpu.make_async_remote_copy(
                src_ref=q_hbm.at[pl.ds(r * part, part), cols], dst_ref=qbuf.at[r, block(at), cols],
                send_sem=qs.at[g, d], recv_sem=qr.at[g, d], device_id=to_chip(d), device_id_type=MESH)

        def q_cross(g, d, at):
            r, lo, hi = groups[g]
            cols = pl.ds(lo * HD, (hi - lo) * HD)
            place = pl.ds(pl.multiple_of(half + lax.rem(chip + chips - at, chips) * part, part), part)
            return pltpu.make_async_remote_copy(
                src_ref=q_hbm.at[pl.ds(r * part, part), cols], dst_ref=qbuf.at[r, place, cols],
                send_sem=xs.at[g, d], recv_sem=xr.at[g, d],
                device_id={"tm": 2 * lax.rem(chip + d, chips) + 1 - core}, device_id_type=MESH)

        def q_pass(g):
            r, lo, hi = groups[g]
            cols = pl.ds(lo * HD, (hi - lo) * HD)
            return pltpu.make_async_remote_copy(
                src_ref=qbuf.at[r, pl.ds(0, half), cols], dst_ref=qbuf.at[r, pl.ds(half, half), cols],
                send_sem=fs.at[g], recv_sem=fr.at[g], device_id={"tm": sibling}, device_id_type=MESH)

        def q_send(g):
            if g < direct:
                q_cross(g, 0, 0).start()

            def one(d):
                q_copy(g, d, 0).start()
                if g < direct:
                    q_cross(g, d, 0).start()
            each(1, chips, one)

        def q_need(g):
            if g < direct:
                each(1, chips, lambda d: q_copy(g, d, d).wait_recv())
                each(0, chips, lambda d: q_cross(g, d, d).wait_recv())
            else:
                q_pass(g).wait_recv()

        def q_relay(g):
            each(1, chips, lambda d: q_copy(g, d, d).wait_recv())
            q_pass(g).start()

        def step(t, cur, nxt, mcur, mnxt):
            h = lax.rem(t, heads)
            hn, rn = lax.rem(t + 1, heads), (t + 1) // heads
            mx, acc = [None, None], [None, None]
            parts = [slice(0, half), slice(half, tile)]
            for c in range(kv // KEYS):
                ck = slice(c * KEYS, (c + 1) * KEYS)
                for i, rs in enumerate(parts):
                    if nxt is not None:
                        qn = qbuf[rn, rs, hcol(hn)]
                        x = lax.dot_general(qn, kbuf[hn, ck, :], NT, preferred_element_type=F32)
                        nxt[rs, ck] = x
                        y = x[:, :HD]
                        for n in range(1, KEYS // HD):
                            y = jnp.maximum(y, x[:, n * HD:(n + 1) * HD])
                        mx[i] = y if c == 0 else jnp.maximum(mx[i], y)
                    if cur is not None:
                        p = jnp.exp2(cur[rs, ck] * scale - mcur[rs, :1]).astype(BF)
                        d = lax.dot_general(p, vbuf[h, ck, :], NN, preferred_element_type=F32)
                        acc[i] = d if c == 0 else acc[i] + d
            if cur is not None:
                for i, put in ((1, give), (0, keep)):
                    total = acc[i][:, HD:]
                    put[t, :, :HD] = acc[i][:, :HD] / total
                    put[t, :, HD:] = mcur[parts[i], :] + jnp.log(total) * LOG2E
                to_sibling(t).start()
            if nxt is not None:
                for i, rs in enumerate(parts):
                    mnxt[rs, :] = jnp.broadcast_to(jnp.max(mx[i], axis=1, keepdims=True) * scale, (half, HD))

        def to_sibling(t):
            return pltpu.make_async_remote_copy(
                src_ref=give.at[t], dst_ref=taken.at[t], send_sem=gs.at[t], recv_sem=gr.at[t],
                device_id={"tm": sibling}, device_id_type=MESH)

        def o_copy(t, d, at):
            return pltpu.make_async_remote_copy(
                src_ref=osend.at[t, lax.rem(chip + d, chips)], dst_ref=orecv.at[t, lax.rem(chip + chips - at, chips)],
                send_sem=os.at[t, d], recv_sem=orr.at[t, d], device_id=to_chip(d), device_id_type=MESH)

        def merge(t):
            to_sibling(t).wait_recv()
            la, lb = keep[t, :, HD:], taken[t, :, HD:]
            top = jnp.maximum(la, lb)
            wa, wb = jnp.exp2(la - top), jnp.exp2(lb - top)
            total = wa + wb
            mean = (wa * keep[t, :, :HD] + wb * taken[t, :, :HD]) / total
            lse = top + jnp.log(total) * LOG2E
            hi = lse.astype(BF).astype(F32)
            mid = (lse - hi).astype(BF).astype(F32)
            low = lse - hi - mid
            lane = lax.broadcasted_iota(jnp.int32, (half, HD), 1)
            stats = jnp.where(lane == 0, hi, jnp.where(lane == 1, mid, jnp.where(lane == 2, low, 0.0)))
            osend[t, :, :, :HD] = mean.astype(BF).reshape(chips, part, HD)
            osend[t, :, :, HD:] = stats.astype(BF).reshape(chips, part, HD)
            each(1, chips, lambda d: o_copy(t, d, 0).start())
            orecv[t, chip] = osend[t, chip]

        def combine(t):
            each(1, chips, lambda d: o_copy(t, d, d).wait_recv())
            stats = orecv[t, :, :, HD:].reshape(half, HD)
            lse = lax.dot_general(stats, jnp.ones((HD, HD), BF), NN, preferred_element_type=F32)
            lse = lse.reshape(chips, part, HD)
            w = jnp.exp2(lse - jnp.max(lse, axis=0, keepdims=True))
            num = jnp.sum(w * orecv[t, :, :, :HD].astype(F32), axis=0)
            att[t // heads, :, hcol(lax.rem(t, heads))] = (num / jnp.sum(w, axis=0)).astype(BF)

        def p_copy(r, d):
            return pltpu.make_async_remote_copy(
                src_ref=psend.at[r, d], dst_ref=precv.at[r, d], send_sem=ps.at[r, d], recv_sem=pr.at[r, d],
                device_id=to_group(d), device_id_type=MESH)

        most = width - HD

        def prepare(r):
            def share(d):
                shares[d] = lax.dot_general(
                    att[r, :, :most], wbuf[:most, fcol(lax.rem(te + d, n_te))], NN, preferred_element_type=F32)
            each(0, n_te, share)

        def project(r):
            def product(d):
                return shares[d] + lax.dot_general(
                    att[r, :, most:], wbuf[most:, fcol(lax.rem(te + d, n_te))], NN, preferred_element_type=F32)

            def share(d):
                psend[r, d] = product(d).astype(BF)
                p_copy(r, d).start()
            each(1, n_te, share)
            out[r * part:(r + 1) * part, :] = product(0)

        def unite(r):
            def add(d):
                p_copy(r, d).wait_recv()
                out[r * part:(r + 1) * part, :] += precv[r, d].astype(F32)
            each(1, n_te, add)

        def before(t):
            h, hn = lax.rem(t, heads), lax.rem(t + 1, heads)
            for g in range(1, len(groups)):
                r, lo, _ = groups[g]

                @pl.when(t + 1 == r * heads + lo)
                def _(g=g):
                    q_need(g)

            @pl.when(t + 1 < heads)
            def _():
                k_load(hn).wait()

            @pl.when(t < heads)
            def _():
                v_load(h).wait()

        def after(t):
            for g in range(direct, len(groups)):
                @pl.when(t == relay_at[g])
                def _(g=g):
                    q_relay(g)

            @pl.when(t >= 1)
            def _():
                merge(t - 1)

            @pl.when(t >= LAG)
            def _():
                combine(t - LAG)

        for g in range(len(groups)):
            q_send(g)
        k_load(0).wait()
        q_need(0)
        step(0 * tm - 1, None, s_a, None, m_a)

        def pair(u, _):
            before(2 * u)
            step(2 * u, s_a, s_b, m_a, m_b)
            after(2 * u)
            before(2 * u + 1)
            step(2 * u + 1, s_b, s_a, m_b, m_a)
            after(2 * u + 1)
            return 0

        last = 0 * tm + steps - 1
        lax.fori_loop(0, (steps - 1) // 2, pair, 0)
        if steps % 2 == 0:
            before(last - 1)
            step(last - 1, s_a, s_b, m_a, m_b)
            after(last - 1)
        end = (s_b, m_b) if steps % 2 == 0 else (s_a, m_a)
        before(last)
        step(last, end[0], None, end[1], None)
        after(last)
        merge(last)
        w_load.wait()
        for r in range(TILES - 1):
            prepare(r)
            project(r)
        for i in range(LAG - 1, 0, -1):
            combine(last - i)
        prepare(TILES - 1)
        combine(last)
        project(TILES - 1)

        def sent(d):
            for g in range(len(groups)):
                q_copy(g, d, 0).wait_send()
                if g < direct:
                    q_cross(g, d, 0).wait_send()
            each(0, steps, lambda t: o_copy(t, d, 0).wait_send())

        each(1, chips, sent)
        for g in range(len(groups)):
            if g < direct:
                q_cross(g, 0, 0).wait_send()
            else:
                q_pass(g).wait_send()
        each(0, steps, lambda t: to_sibling(t).wait_send())
        for r in range(TILES):
            unite(r)
        for r in range(TILES):
            each(1, n_te, lambda d: p_copy(r, d).wait_send())

    any_ = pl.BlockSpec(memory_space=pl.ANY)
    dma = pltpu.SemaphoreType.DMA
    n_g = len(groups)
    return pl.pallas_call(
        kernel,
        out_shape=jax.ShapeDtypeStruct((own, feat), F32),
        in_specs=[any_] * 4,
        out_specs=pl.BlockSpec(memory_space=pltpu.VMEM),
        scratch_shapes=[
            pltpu.VMEM((TILES, tile, width), BF),
            pltpu.VMEM((heads, kv, HD), BF),
            pltpu.VMEM((heads, kv, 2 * HD), BF),
            pltpu.VMEM((width, model), BF),
            pltpu.VMEM((tile, kv), F32),
            pltpu.VMEM((tile, kv), F32),
            pltpu.VMEM((tile, HD), F32),
            pltpu.VMEM((tile, HD), F32),
            pltpu.VMEM((steps, half, 2 * HD), F32),
            pltpu.VMEM((steps, half, 2 * HD), F32),
            pltpu.VMEM((steps, half, 2 * HD), F32),
            pltpu.VMEM((steps, chips, part, 2 * HD), BF),
            pltpu.VMEM((steps, chips, part, 2 * HD), BF),
            pltpu.VMEM((TILES, part, width), BF),
            pltpu.VMEM((n_te, part, feat), F32),
            pltpu.VMEM((TILES, n_te, part, feat), BF),
            pltpu.VMEM((TILES, n_te, part, feat), BF),
            dma((TILES,)), dma((heads,)), dma((heads,)), dma,
            dma((n_g, chips)), dma((n_g, chips)), dma((n_g, chips)), dma((n_g, chips)), dma((n_g,)), dma((n_g,)),
            dma((steps,)), dma((steps,)),
            dma((steps, chips)), dma((steps, chips)),
            dma((TILES, n_te)), dma((TILES, n_te)),
        ],
        compiler_params=pltpu.CompilerParams(
            collective_id=0, has_side_effects=True, vmem_limit_bytes=60 * 2**20),
        name="late_uniting_attention",
    )(queries, cached_keys, cached_values, out_weight)


def solution(mesh):
    placed = (P("tm", "tensor"), P("tm", "tensor"), P("tm", "tensor"), P("tensor", None))
    return jax.shard_map(
        on_device, mesh=mesh, in_specs=placed, out_specs=P("tm", "tensor"), check_vma=False
    )
```
